512 devices in a mesh: segment: 32 (over y, z_hi), tp: 16 (over x, z_lo, core).
Axes of the slice: x: 4, y: 8, z: 8 (z_hi: 4, z_lo: 2; z = z_hi * 2 + z_lo), core: 2. Of those that a mesh axis runs over, the one named last changes fastest.
Arguments:
- residual: bfloat16 [32, 128, 4096], P('segment', 'tp'), may hold values from -6 to 6
- pending: bfloat16 [32, 128, 4096], P('segment', 'tp'), may hold values from -6 to 6
- span_index: int32 [32], P('segment'), may hold values from 0 to 63
- prefix_len: int32 [32], P('segment'), may hold values from 192 to 1536
- norm_gain: bfloat16 [32, 4096], P('segment'), may hold values from 0.099609375 to 1.8984375
- w_query: bfloat16 [32, 4096, 4096], P('segment', None, 'tp'), may hold values from -0.1875 to 0.1875
- w_kv: bfloat16 [32, 4096, 1024], P('segment', None, 'tp'), may hold values from -0.09375 to 0.09375
- w_out: bfloat16 [32, 4096, 4096], P('segment', 'tp'), may hold values from -0.5 to 0.5
- prefix_cache: bfloat16 [32, 6144, 256], P('segment', 'tp'), may hold values from -68 to 68
Outputs:
- carried: bfloat16 [32, 128, 4096], P('segment', 'tp')
- output: bfloat16 [32, 128, 4096], P('segment', 'tp')
The draws below stay inside these ranges and needn't reach their ends.
All inputs are finite; a program needn't handle non-finite values.
Results may differ from the reference program's by a relative error of at most 0.04.
Values may be sent and summed in bfloat16 or wider, within the bound.
No kernel may reach another device: no remote copies, remote signals or barrier semaphores. Data moves between devices by JAX's collectives and lax.ppermute only.
A program may use at most 64 MiB of HBM per device.

```python
import jax
import jax.numpy as jnp
from jax import lax

D = 4096
HEADS = 32
KV_HEADS = 4
HD = 128
SPAN = 128
PREFIX = 1536
TICKS = 2
SECTIONS = 32


def draw_prefix_len(key, part):
    key = jax.random.fold_in(key, 7)
    key_base, key_high, key_low = jax.random.split(key, 3)
    lengths = jax.random.randint(key_base, (SECTIONS,), PREFIX // 8, PREFIX + 1, dtype=jnp.int32)
    high_spot = jax.random.randint(key_high, (), 0, SECTIONS, dtype=jnp.int32)
    low_spot = (high_spot + 1 + jax.random.randint(key_low, (), 0, SECTIONS - 1, dtype=jnp.int32)) % SECTIONS
    lengths = lengths.at[high_spot].set(PREFIX)
    lengths = lengths.at[low_spot].set(PREFIX // 8)
    return lengths


def draw_prefix_cache(key, part):
    key = jax.random.fold_in(key, 11)
    key_base = jax.random.fold_in(key, 0)
    shape_full = (SECTIONS, KV_HEADS * PREFIX, 2 * HD)
    return jnp.clip(jax.random.normal(key_base, shape_full, jnp.float32), -6.0, 6.0).astype(jnp.bfloat16)


def touch_ends(entries, own_key, smallest, largest):
    longest = entries.shape.index(max(entries.shape))
    spots = []
    for shift in (0, 1):
        where = [jax.random.randint(jax.random.fold_in(own_key, axis), (), 0, length) for axis, length in enumerate(entries.shape)]
        where[longest] = (where[longest] + shift) % entries.shape[longest]
        spots.append(tuple(where))
    return entries.at[spots[0]].set(smallest).at[spots[1]].set(largest)


def block_levels(stream_key, dims, pieces, smallest, high):
    def one(axis_at, blocks):
        heights = jax.random.uniform(jax.random.fold_in(jax.random.fold_in(stream_key, 6), axis_at), (blocks,), jnp.float32, smallest / len(pieces), high / len(pieces))
        return jnp.repeat(jnp.exp(heights), dims[axis_at] // blocks).reshape((-1,) + (1,) * (len(dims) - axis_at - 1))

    loudness = one(*pieces[0])
    for cut in pieces[1:]:
        loudness = loudness * one(*cut)
    return loudness


def scatter_about(own_key, shape, scale, limit, cuts=(), held_as=jnp.bfloat16):
    entries = jax.random.normal(own_key, shape, jnp.float32) * scale
    if len(cuts) > 0:
        entries = block_levels(own_key, shape, cuts, -0.22, 0.18) * entries
    return jnp.clip(entries, min=-limit, max=limit).astype(held_as)


def setup_inputs(seed: int = 0) -> dict:
    seeds = jax.random.split(jax.random.key(seed), 10)
    return {
        "residual": scatter_about(seeds[0], (SECTIONS, SPAN, D), 1.0, 6.0, ((0, 32), (1, 16))),
        "pending": scatter_about(seeds[1], (SECTIONS, SPAN, D), 1.0, 6.0, ((0, 32), (1, 16))),
        "span_index": touch_ends(jax.random.randint(seeds[2], (SECTIONS,), 0, 64), jax.random.fold_in(seeds[2], 1), 0, 63).astype(jnp.int32),
        "prefix_len": draw_prefix_len(jax.random.fold_in(seeds[9], 71), 0),
        "norm_gain": jnp.clip(1.0 + 0.18 * jax.random.normal(seeds[4], (SECTIONS, D), jnp.float32), 0.099609375, 1.8984375).astype(jnp.bfloat16),
        "w_query": scatter_about(seeds[5], (SECTIONS, D, HEADS * HD), (D // 4) ** -0.5, 0.1875, ((0, 32), (2, 16))),
        "w_kv": scatter_about(seeds[6], (SECTIONS, D, 2 * KV_HEADS * HD), D ** -0.5, 0.09375, ((0, 32), (2, 16))),
        "w_out": scatter_about(seeds[7], (SECTIONS, HEADS * HD, D), HD ** -0.5, 0.5, ((0, 32), (1, 16))),
        "prefix_cache": draw_prefix_cache(jax.random.fold_in(seeds[9], 71), 0),
    }


norm_eps = 1e-05
rope_base = 500000.0

def rotate(values, positions):
    half_width = values.shape[-1] // 2
    inverse = rope_base ** (-jnp.arange(0, values.shape[-1], 2, dtype=jnp.float32) / values.shape[-1])
    angles = positions.astype(jnp.float32)[:, None] * inverse[None, :]
    cosine_table = jnp.cos(angles)[:, None, :]
    sine_table = jnp.sin(angles)[:, None, :]
    first_half = values[..., :half_width]
    second_half = values[..., half_width:]
    return jnp.concatenate([first_half * cosine_table - second_half * sine_table, second_half * cosine_table + first_half * sine_table], axis=-1)

def section_block(section_items):
    residual_rows, pending_rows, span_number, length, gain_row, query_weight, pair_weight, out_weight, cache_rows = section_items
    widths = residual_rows.astype(jnp.float32)
    mean_square = lax.optimization_barrier(jnp.mean(widths * widths, axis=-1, keepdims=True))
    normed = (widths * lax.rsqrt(mean_square + norm_eps) * gain_row.astype(jnp.float32)).astype(jnp.bfloat16)
    positions = span_number * SPAN + jnp.arange(SPAN, dtype=jnp.int32)
    queries = jnp.dot(normed, query_weight, preferred_element_type=jnp.float32).reshape(SPAN, HEADS, HD)
    queries = rotate(queries, positions).astype(jnp.bfloat16)
    fresh_pairs = jnp.dot(normed, pair_weight, preferred_element_type=jnp.float32).astype(jnp.bfloat16)
    fresh_pairs = fresh_pairs.reshape(SPAN, KV_HEADS, 2, HD)
    new_keys = rotate(fresh_pairs[:, :, 0, :].astype(jnp.float32), positions).astype(jnp.bfloat16)
    new_values = fresh_pairs[:, :, 1, :]
    stored = cache_rows.reshape(KV_HEADS, PREFIX, 2 * HD)
    all_keys = jnp.concatenate([stored[:, :, :HD], jnp.transpose(new_keys, (1, 0, 2))], axis=1)
    all_values = jnp.concatenate([stored[:, :, HD:], jnp.transpose(new_values, (1, 0, 2))], axis=1)
    group_ratio = HEADS // KV_HEADS
    grouped = queries.reshape(SPAN, KV_HEADS, group_ratio, HD).astype(jnp.float32)
    scores = jnp.einsum('cgrd,gkd->grck', grouped, all_keys.astype(jnp.float32)) * HD ** (-0.5)
    slot_index = jnp.arange(PREFIX + SPAN, dtype=jnp.int32)[None, :]
    row_index = jnp.arange(SPAN, dtype=jnp.int32)[:, None]
    allowed = jnp.where(slot_index < PREFIX, slot_index < length, slot_index - PREFIX <= row_index)
    scores = jnp.where(allowed[None, None], scores, -jnp.inf)
    row_peak = lax.optimization_barrier(jnp.max(scores, axis=-1, keepdims=True))
    exp_scores = jnp.exp(scores - row_peak)
    denominator = lax.optimization_barrier(jnp.sum(exp_scores, axis=-1, keepdims=True))
    softmax_weights = (exp_scores / denominator).astype(jnp.bfloat16)
    attended = jnp.einsum('grck,gkd->cgrd', softmax_weights.astype(jnp.float32), all_values.astype(jnp.float32))
    attended = attended.astype(jnp.bfloat16).reshape(SPAN, HEADS * HD)
    output = jnp.dot(attended, out_weight, preferred_element_type=jnp.float32).astype(jnp.bfloat16)
    carried = (widths + pending_rows.astype(jnp.float32)).astype(jnp.bfloat16)
    return (carried, output)

def reference(residual, pending, span_index, prefix_len, norm_gain, w_query, w_kv, w_out, prefix_cache):
    for segment_tick in range(TICKS):
        carried, output = lax.map(section_block, (residual, pending, span_index, prefix_len, norm_gain, w_query, w_kv, w_out, prefix_cache))
        if segment_tick + 1 < TICKS:
            residual = jnp.concatenate([jnp.zeros_like(carried[:1]), carried[:-1]], axis=0)
            pending = jnp.concatenate([jnp.zeros_like(output[:1]), output[:-1]], axis=0)
            span_index = jnp.concatenate([jnp.zeros_like(span_index[:1]), span_index[:-1]], axis=0)
    return (carried, output)
```

```python
import jax
import jax.numpy as jnp
import numpy as np
from jax import lax
from jax.experimental import pallas as pl
from jax.experimental.pallas import tpu as pltpu
from jax.sharding import PartitionSpec as P

KV_HEADS = 4
HD = 128
SPAN = 128
PREFIX = 1536
SPANS = 64
norm_eps = 1e-05
rope_base = 500000.0
MIB = 1 << 20


def rope_tables():
    inverse = rope_base ** (-np.arange(0, HD, 2, dtype=np.float64) / HD)
    inverse = np.concatenate([inverse, inverse])
    chips, ticks, tokens = SPAN // 16, 2, 8
    place = np.arange(chips)[None, :, None, None] * 2 + np.arange(2)[:, None, None, None]
    token = place * tokens + np.arange(tokens)[None, None, None, :]
    token = np.broadcast_to(token, (2, chips, ticks, tokens)).reshape(2, SPAN, 1)
    start = np.arange(SPANS)[:, None] * SPAN
    return [
        np.asarray(f(p * inverse), np.float32) for p in (token, start) for f in (np.cos, np.sin)
    ]


def norm_kernel(residual_ref, earlier_ref, gain_ref, out_ref):
    gain = gain_ref[...].astype(jnp.float32)
    rows = jnp.concatenate(
        [residual_ref[...].astype(jnp.float32), earlier_ref[...].astype(jnp.float32)], axis=0
    )
    mean_square = jnp.mean(rows * rows, axis=-1, keepdims=True)
    normed = (rows * lax.rsqrt(mean_square + norm_eps) * gain).astype(jnp.bfloat16)
    for copy in range(out_ref.shape[0]):
        out_ref[copy] = normed


def project_kernel(
    info_ref, own_ref, other_ref, wq_ref, wkv_ref, cos_tok, sin_tok, cos_span, sin_span,
    q_ref, kv_ref, q_acc, kv_acc,
):
    step = pl.program_id(0)

    @pl.when(step == 0)
    def _():
        q_acc[...] = jnp.zeros_like(q_acc)
        kv_acc[...] = jnp.zeros_like(kv_acc)

    rows = jnp.concatenate([own_ref[...], other_ref[...]], axis=0)
    q_acc[...] += jnp.dot(rows, wq_ref[...], preferred_element_type=jnp.float32)
    kv_acc[...] += lax.dot_general(
        rows, wkv_ref[...], (((1,), (1,)), ((), ())), preferred_element_type=jnp.float32
    )

    @pl.when(step == pl.num_programs(0) - 1)
    def _():
        core, z_place = info_ref[3], info_ref[4]
        row = lax.broadcasted_iota(jnp.int32, (SPAN, HD), 0)
        lane = lax.broadcasted_iota(jnp.int32, (SPAN, HD), 1)
        early = (row // 8) % 2 == 0
        cos_a = jnp.where(early, cos_span[pl.ds(info_ref[0], 1), :], cos_span[pl.ds(info_ref[1], 1), :])
        sin_a = jnp.where(early, sin_span[pl.ds(info_ref[0], 1), :], sin_span[pl.ds(info_ref[1], 1), :])
        for half in range(2):
            side = core if half == 0 else 1 - core
            cos_b, sin_b = cos_tok[side], sin_tok[side]
            cosine = cos_b * cos_a - sin_b * sin_a
            sine = sin_b * cos_a + cos_b * sin_a
            sine = jnp.where(lane < HD // 2, -sine, sine)
            here = pl.ds(half * SPAN, SPAN)

            def rotated(values):
                return (values * cosine + pltpu.roll(values, HD // 2, 1) * sine).astype(jnp.bfloat16)

            for head in range(q_ref.shape[1] // HD):
                columns = pl.ds(head * HD, HD)
                q_ref[here, columns] = rotated(q_acc[here, columns])
            pairs = kv_acc[here, :].astype(jnp.bfloat16)
            keys = rotated(pairs.astype(jnp.float32))
            kv_ref[here, :] = jnp.where(z_place == 0, keys, pairs)


def attend_kernel(info_ref, q_ref, kv_own_ref, kv_other_ref, cache_ref, wout_ref, att_ref, part_ref):
    length, core, z_place = info_ref[2], info_ref[3], info_ref[4]
    kv_own, kv_other = kv_own_ref[...], kv_other_ref[...]
    new_keys = jnp.where(z_place == 0, kv_own, kv_other)
    new_values = jnp.where(z_place == 0, kv_other, kv_own)
    rows = 2 * SPAN

    def place(index):
        half = index // SPAN
        side = jnp.where(half == 0, core, 1 - core)
        token = (((index // 16) % 8) * 2 + side) * 8 + index % 8
        return (index // 8) % 2, token

    row_tick, row_token = place(lax.broadcasted_iota(jnp.int32, (rows, 1), 0))
    key_tick, key_token = place(lax.broadcasted_iota(jnp.int32, (1, rows), 1))
    fresh = (row_tick == key_tick) & (key_token <= row_token)
    slots = lax.broadcasted_iota(jnp.int32, (1, PREFIX), 1)
    cached = slots < length
    contract = (((1,), (1,)), ((), ()))
    for head in range(q_ref.shape[1] // HD):
        columns = pl.ds(head * HD, HD)
        queries = q_ref[:, columns]
        s_prefix = lax.dot_general(
            queries, cache_ref[:, pl.ds(0, HD)], contract, preferred_element_type=jnp.float32
        )
        s_fresh = lax.dot_general(queries, new_keys, contract, preferred_element_type=jnp.float32)
        scale = HD ** (-0.5)
        s_prefix = jnp.where(cached, s_prefix * scale, -jnp.inf)
        s_fresh = jnp.where(fresh, s_fresh * scale, -jnp.inf)
        peak = jnp.maximum(
            jnp.max(s_prefix, axis=-1, keepdims=True), jnp.max(s_fresh, axis=-1, keepdims=True)
        )
        e_prefix = jnp.exp(s_prefix - peak)
        e_fresh = jnp.exp(s_fresh - peak)
        total = jnp.sum(e_prefix, axis=-1, keepdims=True) + jnp.sum(e_fresh, axis=-1, keepdims=True)
        summed = jnp.dot(
            e_prefix.astype(jnp.bfloat16), cache_ref[:, pl.ds(HD, HD)], preferred_element_type=jnp.float32
        ) + jnp.dot(e_fresh.astype(jnp.bfloat16), new_values, preferred_element_type=jnp.float32)
        att_ref[:, columns] = (summed / total).astype(jnp.bfloat16)
    part_ref[...] = jnp.dot(
        att_ref[pl.ds(SPAN, SPAN), :], wout_ref[...], preferred_element_type=jnp.float32
    ).astype(jnp.bfloat16)


def out_kernel(att_ref, wout_ref, part_ref):
    part_ref[...] = jnp.dot(att_ref[...], wout_ref[...], preferred_element_type=jnp.float32)


def swapped(array, bit):
    return lax.ppermute(array, "tp", [(i, i ^ bit) for i in range(lax.axis_size("tp"))])


def to_next_section(array):
    sections = lax.axis_size("segment")
    return lax.ppermute(array, "segment", [(i, i + 1) for i in range(sections - 1)])


def shards(
    residual, pending, span_index, prefix_len, norm_gain, w_query, w_kv, w_out, prefix_cache
):
    tp_size = lax.axis_size("tp")
    tp_place = lax.axis_index("tp")
    core, z_place = tp_place % 2, tp_place // 2 % 2
    width = residual.shape[2]
    tokens = residual.shape[1]
    chips = tp_size // 2
    same_core = [list(range(c, tp_size, 2)) for c in range(2)]
    same_chip = [[i, i + 1] for i in range(0, tp_size, 2)]
    same_head = [list(range(i, i + 4)) for i in range(0, tp_size, 4)]
    vmem = pl.BlockSpec(memory_space=pltpu.VMEM)
    smem = pl.BlockSpec(memory_space=pltpu.SMEM)

    cache = lax.all_gather(prefix_cache[0], "tp", axis=0, tiled=True, axis_index_groups=same_head)
    pair_weight = lax.all_gather(
        jnp.transpose(w_kv[0]), "tp", axis=0, tiled=True, axis_index_groups=same_chip
    )

    carried = (residual[0].astype(jnp.float32) + pending[0].astype(jnp.float32)).astype(jnp.bfloat16)
    index_lanes = jnp.broadcast_to(span_index.astype(jnp.bfloat16)[:, None], (tokens, HD))
    earlier = to_next_section(jnp.concatenate([carried, index_lanes], axis=1))
    earlier_index = earlier[0, width].astype(jnp.int32)
    earlier = earlier[:, :width]
    info = jnp.stack([span_index[0], earlier_index, prefix_len[0], core, z_place])

    normed = pl.pallas_call(
        norm_kernel,
        out_shape=jax.ShapeDtypeStruct((chips, 2 * tokens, width), jnp.bfloat16),
        in_specs=[vmem, vmem, vmem],
        out_specs=vmem,
        compiler_params=pltpu.CompilerParams(vmem_limit_bytes=16 * MIB),
    )(residual[0], earlier, norm_gain)
    own = lax.all_to_all(normed, "tp", 0, 0, axis_index_groups=same_core)
    own = own.reshape(SPAN, width)
    other = swapped(own, 1)

    steps = 4
    depth = width // steps
    columns = w_query.shape[2]
    tables = [jnp.asarray(t) for t in rope_tables()]
    whole = lambda a: pl.BlockSpec(a.shape, lambda k: (0,) * a.ndim)
    q, pairs = pl.pallas_call(
        project_kernel,
        grid=(steps,),
        out_shape=[
            jax.ShapeDtypeStruct((2 * SPAN, columns), jnp.bfloat16),
            jax.ShapeDtypeStruct((2 * SPAN, HD), jnp.bfloat16),
        ],
        in_specs=[
            smem,
            pl.BlockSpec((SPAN, depth), lambda k: (0, k)),
            pl.BlockSpec((SPAN, depth), lambda k: (0, k)),
            pl.BlockSpec((depth, columns), lambda k: (k, 0)),
            pl.BlockSpec((HD, depth), lambda k: (0, k)),
        ]
        + [whole(t) for t in tables],
        out_specs=[
            pl.BlockSpec((2 * SPAN, columns), lambda k: (0, 0)),
            pl.BlockSpec((2 * SPAN, HD), lambda k: (0, 0)),
        ],
        scratch_shapes=[
            pltpu.VMEM((2 * SPAN, columns), jnp.float32),
            pltpu.VMEM((2 * SPAN, HD), jnp.float32),
        ],
        compiler_params=pltpu.CompilerParams(vmem_limit_bytes=24 * MIB),
    )(info, own, other, w_query[0], pair_weight, *tables)
    other_pairs = swapped(pairs, 2)

    attended, part_other = pl.pallas_call(
        attend_kernel,
        out_shape=[
            jax.ShapeDtypeStruct((2 * SPAN, columns), jnp.bfloat16),
            jax.ShapeDtypeStruct((SPAN, width), jnp.bfloat16),
        ],
        in_specs=[smem, vmem, vmem, vmem, vmem, vmem],
        out_specs=[vmem, vmem],
        compiler_params=pltpu.CompilerParams(vmem_limit_bytes=32 * MIB),
    )(info, q, pairs, other_pairs, cache, w_out[0])
    arrived = swapped(part_other, 1)
    part_own = pl.pallas_call(
        out_kernel,
        out_shape=jax.ShapeDtypeStruct((SPAN, width), jnp.float32),
        in_specs=[vmem, vmem],
        out_specs=vmem,
        compiler_params=pltpu.CompilerParams(vmem_limit_bytes=24 * MIB),
        cost_estimate=pl.CostEstimate(
            flops=2 * SPAN * columns * width, bytes_accessed=8 * MIB, transcendentals=0
        ),
    )(attended[:SPAN], w_out[0])
    chip_part = (part_own + arrived.astype(jnp.float32)).astype(jnp.bfloat16)
    parts = lax.all_to_all(
        chip_part.reshape(chips, 2 * tokens, width), "tp", 0, 0, axis_index_groups=same_core
    )
    summed = jnp.sum(parts.astype(jnp.float32), axis=0).astype(jnp.bfloat16)
    late_output = to_next_section(summed[:tokens])
    final_carried = (earlier.astype(jnp.float32) + late_output.astype(jnp.float32)).astype(jnp.bfloat16)
    return (final_carried[None], summed[tokens:][None])


def solution(mesh):
    in_specs = (
        P("segment", "tp", None),
        P("segment", "tp", None),
        P("segment"),
        P("segment"),
        P("segment", None),
        P("segment", None, "tp"),
        P("segment", None, "tp"),
        P("segment", "tp", None),
        P("segment", "tp", None),
    )
    out_specs = (P("segment", "tp", None), P("segment", "tp", None))
    return jax.shard_map(shards, mesh=mesh, in_specs=in_specs, out_specs=out_specs, check_vma=False)
```

```python
import functools

import jax
import jax.numpy as jnp
import numpy as np
from jax import lax
from jax.experimental import pallas as pl
from jax.experimental.pallas import tpu as pltpu
from jax.sharding import PartitionSpec as P

KV_HEADS = 4
HD = 128
SPAN = 128
PREFIX = 1536
SPANS = 64
norm_eps = 1e-05
rope_base = 500000.0
MIB = 1 << 20


contract_last = (((1,), (1,)), ((), ()))


def rope_tables():
    inverse = rope_base ** (-np.arange(0, HD, 2, dtype=np.float64) / HD)
    inverse = np.concatenate([inverse, inverse])
    chips, tokens = SPAN // 16, 8
    place = np.arange(chips)[None, :, None] * 2 + np.arange(2)[:, None, None]
    token = (place * tokens + np.arange(tokens)[None, None, :]).reshape(2, SPAN // 2, 1)
    start = np.arange(SPANS)[:, None] * SPAN
    return [
        np.asarray(f(p * inverse), np.float32) for p in (token, start) for f in (np.cos, np.sin)
    ]


def carry_kernel(span_ref, residual_ref, pending_ref, out_ref):
    tokens, width = residual_ref.shape
    carried = residual_ref[...].astype(jnp.float32) + pending_ref[...].astype(jnp.float32)
    out_ref[:, :width] = carried.astype(jnp.bfloat16)
    index = jnp.full((tokens, out_ref.shape[1] - width), span_ref[0], jnp.int32)
    out_ref[:, width:] = index.astype(jnp.float32).astype(jnp.bfloat16)


def normalised(rows_ref, gain_ref):
    rows = rows_ref[:, : gain_ref.shape[1]].astype(jnp.float32)
    mean_square = jnp.mean(rows * rows, axis=-1, keepdims=True)
    return rows * lax.rsqrt(mean_square + norm_eps) * gain_ref[...].astype(jnp.float32)


def norm_kernel(residual_ref, earlier_ref, gain_ref, out_ref):
    ticks = [normalised(ref, gain_ref) for ref in (residual_ref, earlier_ref)]
    normed = jnp.concatenate(ticks, axis=0).astype(jnp.bfloat16)
    for copy in range(out_ref.shape[0]):
        out_ref[copy] = normed


def table_kernel(span_ref, info_ref, earlier_ref, cos_tok, sin_tok, cos_span, sin_span, out_ref):
    core = info_ref[0]
    late = earlier_ref[:, -HD:].astype(jnp.float32)[:1].astype(jnp.int32)
    spans = lax.broadcasted_iota(jnp.int32, cos_span.shape, 0)
    low = lax.broadcasted_iota(jnp.int32, out_ref.shape[2:], 1) < HD // 2
    cos_b, sin_b = cos_tok[core], sin_tok[core]
    for tick, index in enumerate((span_ref[0], late)):
        cos_a, sin_a = [
            jnp.sum(jnp.where(spans == index, table[...], 0.0), axis=0, keepdims=True)
            for table in (cos_span, sin_span)
        ]
        sine = sin_b * cos_a + cos_b * sin_a
        out_ref[0, tick] = cos_b * cos_a - sin_b * sin_a
        out_ref[1, tick] = jnp.where(low, -sine, sine)


def of_tick(values, tick):
    rows = values.shape[0] // 2
    return values.reshape(rows // 8, 2, 8, HD)[:, tick].reshape(rows, HD)


def rotated(values, table_ref, tick):
    turned = pltpu.roll(values, HD // 2, 1) * table_ref[1, tick]
    return (values * table_ref[0, tick] + turned).astype(jnp.bfloat16)


def query_kernel(rows_ref, weight_ref, table_ref, q_ref):
    queries = jnp.dot(rows_ref[...], weight_ref[...], preferred_element_type=jnp.float32)
    rows = rows_ref.shape[0] // 2
    for tick in range(2):
        for head in range(queries.shape[1] // HD):
            values = of_tick(queries[:, head * HD : (head + 1) * HD], tick)
            q_ref[tick, pl.ds(head * rows, rows), :] = rotated(values, table_ref, tick)


def pair_kernel(info_ref, rows_ref, own_ref, other_ref, table_ref, kv_ref):
    core, z_place = info_ref[0], info_ref[1]
    weight = jnp.concatenate([own_ref[...], other_ref[...]], axis=0)
    pairs = lax.dot_general(
        rows_ref[...], weight, contract_last, preferred_element_type=jnp.float32
    )
    pairs = jnp.where(core == 0, pairs, pltpu.roll(pairs, HD // 2, 1))
    for tick in range(2):
        both = of_tick(pairs, tick).astype(jnp.bfloat16)
        keys = rotated(both.astype(jnp.float32), table_ref, tick)
        for copy in range(kv_ref.shape[0]):
            kv_ref[copy, tick] = jnp.where(z_place == 0, keys, both)


def attend_kernel(
    length_ref, info_ref, q_own, q_other, kv_ref, own, from_z, from_core, from_both,
    wout_own_any, wout_other_any, out_ref, wout_ref, sems,
):
    weight_copies = [
        pltpu.make_async_copy(source, wout_ref.at[side], sems.at[side])
        for side, source in enumerate((wout_own_any, wout_other_any))
    ]
    for copy in weight_copies:
        copy.start()
    core, z_place = info_ref[0], info_ref[1]
    chips, tokens, width = out_ref.shape
    rows = chips * tokens
    queries = jnp.concatenate([q_own[0], q_other[0]], axis=0)

    def token(index, side):
        return ((index % rows // tokens) * 2 + side) * tokens + index % tokens

    row_token = token(lax.broadcasted_iota(jnp.int32, (queries.shape[0], 1), 0), core)
    key = lax.broadcasted_iota(jnp.int32, (1, 2 * rows), 1)
    allowed = [token(key, key // rows) <= row_token]
    keys = [jnp.concatenate([kv_ref[0, 0], kv_ref[1, 0]], axis=0)]
    values = [jnp.concatenate([kv_ref[2, 0], kv_ref[3, 0]], axis=0)]
    block = own.shape[0]
    slot = lax.broadcasted_iota(jnp.int32, (1, block), 1)
    places = [(z, c) for c in (core, 1 - core) for z in (z_place, 1 - z_place)]
    for cache_ref, (z, c) in zip((own, from_z, from_core, from_both), places):
        keys.append(cache_ref[:, :HD])
        values.append(cache_ref[:, HD:])
        allowed.append((z * 2 + c) * block + slot < length_ref[0])

    scores = []
    for key, seen in zip(keys, allowed):
        score = lax.dot_general(queries, key, contract_last, preferred_element_type=jnp.float32)
        scores.append(jnp.where(seen, score * HD ** (-0.5), -jnp.inf))
    peak = functools.reduce(jnp.maximum, [jnp.max(s, axis=-1, keepdims=True) for s in scores])
    total, summed = 0.0, 0.0
    for score, value in zip(scores, values):
        weights = jnp.exp(score - peak)
        total += jnp.sum(weights, axis=-1, keepdims=True)
        summed += jnp.dot(weights.astype(jnp.bfloat16), value, preferred_element_type=jnp.float32)
    result = (summed / total).astype(jnp.bfloat16)
    heads = [result[at : at + rows] for at in range(0, queries.shape[0], rows)]
    half = len(heads) // 2
    sides = [jnp.concatenate(heads[:half], axis=1), jnp.concatenate(heads[half:], axis=1)]
    for copy in weight_copies:
        copy.wait()
    step = 1024
    for left in range(0, width, step):
        columns = pl.ds(left, step)
        part = sum(
            jnp.dot(sides[side], wout_ref[side, :, columns], preferred_element_type=jnp.float32)
            for side in range(2)
        )
        out_ref[:, :, columns] = part.reshape(chips, tokens, step).astype(jnp.bfloat16)


def swapped(array, bit):
    return lax.ppermute(array, "tp", [(i, i ^ bit) for i in range(lax.axis_size("tp"))])


def to_next_section(array):
    sections = lax.axis_size("segment")
    return lax.ppermute(array, "segment", [(i, i + 1) for i in range(sections - 1)])


def after(*arrays):
    return lax.optimization_barrier(arrays)


def shards(
    residual, pending, span_index, prefix_len, norm_gain, w_query, w_kv, w_out, prefix_cache
):
    tp_size = lax.axis_size("tp")
    tp_place = lax.axis_index("tp")
    info = jnp.stack([tp_place % 2, tp_place // 2 % 2])
    tokens, width = residual.shape[1:]
    chips = tp_size // 2
    rows = chips * tokens
    local = w_query.shape[2]
    heads = 2 * local // HD
    same_core = [list(range(c, tp_size, 2)) for c in range(2)]
    same_head = [list(range(i, i + 4)) for i in range(0, tp_size, 4)]
    smem = pl.BlockSpec(memory_space=pltpu.SMEM)
    hbm = pl.BlockSpec(memory_space=pl.ANY)
    bf16, f32 = jnp.bfloat16, jnp.float32
    cos_tok, sin_tok, cos_span, sin_span = [jnp.asarray(t) for t in rope_tables()]

    def block(shape, place=None):
        place = place or (0,) * len(shape)
        return pl.BlockSpec(shape, lambda step: place)

    def kernel(body, inputs, outs, limit, flops=1 << 20, specs=None, scratch=()):
        specs = specs or [smem if a.ndim == 1 else block(a.shape) for a in inputs]
        return pl.pallas_call(
            body,
            grid=(1,),
            out_shape=[jax.ShapeDtypeStruct(shape, dtype) for shape, dtype in outs],
            in_specs=specs,
            out_specs=[block(shape) for shape, _ in outs],
            scratch_shapes=scratch,
            compiler_params=pltpu.CompilerParams(vmem_limit_bytes=limit * MIB),
            cost_estimate=pl.CostEstimate(flops=flops, bytes_accessed=flops // 64, transcendentals=0),
        )(*inputs)

    (carried,) = kernel(
        carry_kernel, [span_index, residual[0], pending[0]], [((tokens, width + HD), bf16)], 60
    )
    earlier = to_next_section(carried)
    cache_z = swapped(prefix_cache[0], 2)
    (normed,) = kernel(
        norm_kernel,
        [residual[0], earlier, norm_gain],
        [((chips, 2 * tokens, width), bf16)],
        60,
        10 * 10**9,
    )
    normed, cache_z = after(normed, cache_z)
    gathered = lax.all_to_all(normed, "tp", 0, 0, axis_index_groups=same_core)
    gathered = gathered.reshape(2 * rows, width)

    _, late_earlier = after(normed, earlier)
    (table,) = kernel(
        table_kernel,
        [span_index, info, late_earlier, cos_tok, sin_tok, cos_span, sin_span],
        [((2, 2, rows, HD), f32)],
        16,
        flops=0,
    )
    _, pair_weight, own_w_query, own_w_out, cache_own, cache_z = after(
        normed, jnp.transpose(w_kv[0]), w_query[0], w_out[0], prefix_cache[0], cache_z
    )
    other_pair_weight = swapped(pair_weight, 1)
    other_w_query = swapped(own_w_query, 1)
    caches = [cache_own, cache_z, swapped(cache_own, 1), swapped(cache_z, 1)]
    other_w_out = swapped(own_w_out, 1)

    (pairs,) = kernel(
        pair_kernel,
        [info, gathered, pair_weight, other_pair_weight, table],
        [((4, 2, rows, HD), bf16)],
        24,
        8 * 10**9,
    )
    pairs = lax.all_to_all(pairs, "tp", 0, 0, axis_index_groups=same_head)
    queries = [
        kernel(
            query_kernel,
            [gathered, weight, table],
            [((2, heads // 2 * rows, HD), bf16)],
            24,
            4 * rows * width * local,
        )[0]
        for weight in (own_w_query, other_w_query)
    ]
    def partial_output(tick):
        half = block((1, heads // 2 * rows, HD), (tick, 0, 0))
        pair = block((4, 1, rows, HD), (0, tick, 0, 0))
        cache = block(cache_own.shape)
        return kernel(
            attend_kernel,
            [prefix_len, info, *queries, pairs, *caches, own_w_out, other_w_out],
            [((chips, tokens, width), bf16)],
            24,
            2 * rows * heads * HD * (width + 2 * PREFIX),
            [smem] * 2 + [half] * 2 + [pair] + [cache] * 4 + [hbm] * 2,
            [pltpu.VMEM((2, *own_w_out.shape), bf16), pltpu.SemaphoreType.DMA((2,))],
        )[0]

    def collected(partial):
        partial = lax.all_to_all(partial, "tp", 0, 0, axis_index_groups=same_core)
        return jnp.sum(partial.astype(f32), axis=0).astype(bf16)

    early_output = to_next_section(collected(partial_output(0)))
    output = collected(partial_output(1))
    final_carried = (earlier[:, :width].astype(f32) + early_output.astype(f32)).astype(bf16)
    return (final_carried[None], output[None])


def solution(mesh):
    in_specs = (
        P("segment", "tp", None),
        P("segment", "tp", None),
        P("segment"),
        P("segment"),
        P("segment", None),
        P("segment", None, "tp"),
        P("segment", None, "tp"),
        P("segment", "tp", None),
        P("segment", "tp", None),
    )
    out_specs = (P("segment", "tp", None), P("segment", "tp", None))
    return jax.shard_map(shards, mesh=mesh, in_specs=in_specs, out_specs=out_specs, check_vma=False)
```

```python
import functools

import jax
import jax.numpy as jnp
import numpy as np
from jax import lax
from jax.experimental import pallas as pl
from jax.experimental.pallas import tpu as pltpu
from jax.sharding import PartitionSpec as P

KV_HEADS = 4
HD = 128
SPAN = 128
PREFIX = 1536
SPANS = 64
norm_eps = 1e-05
rope_base = 500000.0
MIB = 1 << 20


contract_last = (((1,), (1,)), ((), ()))


def rope_tables():
    inverse = rope_base ** (-np.arange(0, HD, 2, dtype=np.float64) / HD)
    inverse = np.concatenate([inverse, inverse])
    chips, tokens = SPAN // 16, 8
    place = np.arange(chips)[None, :, None] * 2 + np.arange(2)[:, None, None]
    token = (place * tokens + np.arange(tokens)[None, None, :]).reshape(2, SPAN // 2, 1)
    start = np.arange(SPANS)[:, None] * SPAN
    return [
        np.asarray(f(p * inverse), np.float32) for p in (token, start) for f in (np.cos, np.sin)
    ]


def carry_kernel(span_ref, residual_ref, pending_ref, out_ref):
    tokens, width = residual_ref.shape
    carried = residual_ref[...].astype(jnp.float32) + pending_ref[...].astype(jnp.float32)
    out_ref[:, :width] = carried.astype(jnp.bfloat16)
    index = span_ref[...].astype(jnp.float32).astype(jnp.bfloat16)
    out_ref[:, width:] = jnp.broadcast_to(index, (tokens, out_ref.shape[1] - width))


def normalised(rows_ref, gain_ref):
    rows = rows_ref[:, : gain_ref.shape[1]].astype(jnp.float32)
    mean_square = jnp.mean(rows * rows, axis=-1, keepdims=True)
    return rows * lax.rsqrt(mean_square + norm_eps) * gain_ref[...].astype(jnp.float32)


def norm_kernel(residual_ref, earlier_ref, gain_ref, out_ref):
    ticks = [normalised(ref, gain_ref) for ref in (residual_ref, earlier_ref)]
    normed = jnp.concatenate(ticks, axis=0).astype(jnp.bfloat16)
    for copy in range(out_ref.shape[0]):
        out_ref[copy] = normed


def table_kernel(info_ref, span_ref, earlier_ref, cos_tok, sin_tok, cos_span, sin_span, out_ref):
    core = info_ref[0]
    late = earlier_ref[:, -HD:].astype(jnp.float32)[:1].astype(jnp.int32)
    spans = lax.broadcasted_iota(jnp.int32, cos_span.shape, 0)
    low = lax.broadcasted_iota(jnp.int32, out_ref.shape[2:], 1) < HD // 2
    cos_b, sin_b = cos_tok[core], sin_tok[core]
    for tick, index in enumerate((span_ref[...], late)):
        cos_a, sin_a = [
            jnp.sum(jnp.where(spans == index, table[...], 0.0), axis=0, keepdims=True)
            for table in (cos_span, sin_span)
        ]
        sine = sin_b * cos_a + cos_b * sin_a
        out_ref[0, tick] = cos_b * cos_a - sin_b * sin_a
        out_ref[1, tick] = jnp.where(low, -sine, sine)


def of_tick(values, tick):
    rows = values.shape[0] // 2
    return values.reshape(rows // 8, 2, 8, HD)[:, tick].reshape(rows, HD)


def rotated(values, table_ref, tick):
    turned = pltpu.roll(values, HD // 2, 1) * table_ref[1, tick]
    return (values * table_ref[0, tick] + turned).astype(jnp.bfloat16)


def query_kernel(rows_ref, own_hbm, other_hbm, table_ref, q_ref, weight_ref, sems):
    slices = []
    for side, weight_hbm in enumerate((own_hbm, other_hbm)):
        for head in range(weight_hbm.shape[1] // HD):
            columns = pl.ds(head * HD, HD)
            at = len(slices)
            slices.append(
                pltpu.make_async_copy(
                    weight_hbm.at[:, columns], weight_ref.at[side, :, columns], sems.at[at]
                )
            )
            slices[at].start()
    rows = rows_ref.shape[0] // 2
    heads = len(slices) // 2
    for at in range(len(slices)):
        slices[at].wait()
        weight = weight_ref[at // heads, :, at % heads * HD : (at % heads + 1) * HD]
        queries = jnp.dot(rows_ref[...], weight, preferred_element_type=jnp.float32)
        for tick in range(2):
            values = of_tick(queries, tick)
            q_ref[tick, pl.ds(at * rows, rows), :] = rotated(values, table_ref, tick)


def pair_kernel(info_ref, rows_ref, own_ref, other_ref, table_ref, kv_ref):
    core, z_place = info_ref[0], info_ref[1]
    weight = jnp.concatenate([own_ref[...], other_ref[...]], axis=0)
    pairs = lax.dot_general(
        rows_ref[...], weight, contract_last, preferred_element_type=jnp.float32
    )
    pairs = jnp.where(core == 0, pairs, pltpu.roll(pairs, HD // 2, 1))
    for tick in range(2):
        both = of_tick(pairs, tick).astype(jnp.bfloat16)
        keys = rotated(both.astype(jnp.float32), table_ref, tick)
        for copy in range(kv_ref.shape[0]):
            kv_ref[copy, tick] = jnp.where(z_place == 0, keys, both)


def attend_kernel(
    info_ref, length_ref, kv_ref, wout_own, q_hbm, own, from_z, from_core, from_both, wout_hbm,
    out_ref, q_ref, cache_ref, wout_other, sems, *, tick,
):
    copies = [pltpu.make_async_copy(q_hbm.at[tick], q_ref, sems.at[0])]
    for at, cache in enumerate((own, from_z, from_core, from_both)):
        copies.append(pltpu.make_async_copy(cache, cache_ref.at[at], sems.at[1 + at]))
    copies.append(pltpu.make_async_copy(wout_hbm, wout_other, sems.at[5]))
    for copy in copies:
        copy.start()
    for copy in copies[:5]:
        copy.wait()
    core, z_place = info_ref[0], info_ref[1]
    chips, tokens, width = out_ref.shape
    rows = chips * tokens
    queries = q_ref[...]

    def token(index, side):
        return ((index % rows // tokens) * 2 + side) * tokens + index % tokens

    row_token = token(lax.broadcasted_iota(jnp.int32, (queries.shape[0], 1), 0), core)
    key = lax.broadcasted_iota(jnp.int32, (1, 2 * rows), 1)
    allowed = [token(key, key // rows) <= row_token]
    keys = [jnp.concatenate([kv_ref[0, 0], kv_ref[1, 0]], axis=0)]
    values = [jnp.concatenate([kv_ref[2, 0], kv_ref[3, 0]], axis=0)]
    block = cache_ref.shape[1]
    slot = lax.broadcasted_iota(jnp.int32, (1, block), 1)
    places = [(z, c) for c in (core, 1 - core) for z in (z_place, 1 - z_place)]
    for at, (z, c) in enumerate(places):
        keys.append(cache_ref[at, :, :HD])
        values.append(cache_ref[at, :, HD:])
        allowed.append((z * 2 + c) * block + slot < length_ref[...])

    scores = []
    for key, seen in zip(keys, allowed):
        score = lax.dot_general(queries, key, contract_last, preferred_element_type=jnp.float32)
        scores.append(jnp.where(seen, score * HD ** (-0.5), -jnp.inf))
    peak = functools.reduce(jnp.maximum, [jnp.max(s, axis=-1, keepdims=True) for s in scores])
    total, summed = 0.0, 0.0
    for score, value in zip(scores, values):
        weights = jnp.exp(score - peak)
        total += jnp.sum(weights, axis=-1, keepdims=True)
        summed += jnp.dot(weights.astype(jnp.bfloat16), value, preferred_element_type=jnp.float32)
    result = (summed / total).astype(jnp.bfloat16)
    heads = [result[at : at + rows] for at in range(0, queries.shape[0], rows)]
    half = len(heads) // 2
    sides = [jnp.concatenate(heads[:half], axis=1), jnp.concatenate(heads[half:], axis=1)]
    copies[5].wait()
    step = 1024
    for left in range(0, width, step):
        columns = pl.ds(left, step)
        part = sum(
            jnp.dot(side, wout_ref[:, columns], preferred_element_type=jnp.float32)
            for side, wout_ref in zip(sides, (wout_own, wout_other))
        )
        out_ref[:, :, columns] = part.reshape(chips, tokens, step).astype(jnp.bfloat16)


def swapped(array, bit):
    return lax.ppermute(array, "tp", [(i, i ^ bit) for i in range(lax.axis_size("tp"))])


def to_next_section(array):
    sections = lax.axis_size("segment")
    return lax.ppermute(array, "segment", [(i, i + 1) for i in range(sections - 1)])


def after(*arrays):
    return lax.optimization_barrier(arrays)


def shards(
    residual, pending, span_index, prefix_len, norm_gain, w_query, w_kv, w_out, prefix_cache
):
    tp_size = lax.axis_size("tp")
    tp_place = lax.axis_index("tp")
    info = jnp.stack([tp_place % 2, tp_place // 2 % 2])
    tokens, width = residual.shape[1:]
    chips = tp_size // 2
    rows = chips * tokens
    local = w_query.shape[2]
    heads = 2 * local // HD
    same_core = [list(range(c, tp_size, 2)) for c in range(2)]
    same_head = [list(range(i, i + 4)) for i in range(0, tp_size, 4)]
    smem = pl.BlockSpec(memory_space=pltpu.SMEM)
    bf16, f32 = jnp.bfloat16, jnp.float32
    cos_tok, sin_tok, cos_span, sin_span = [jnp.asarray(t) for t in rope_tables()]

    def block(shape, place=None):
        place = place or (0,) * len(shape)
        return pl.BlockSpec(shape, lambda step: place)

    def kernel(body, inputs, outs, limit, flops=1 << 20, specs=None, scratch=()):
        specs = specs or [smem if a.ndim == 1 else block(a.shape) for a in inputs]
        return pl.pallas_call(
            body,
            grid=(1,),
            out_shape=outs,
            in_specs=specs,
            out_specs=[block(out.shape) for out in outs],
            scratch_shapes=scratch,
            compiler_params=pltpu.CompilerParams(vmem_limit_bytes=limit * MIB),
            cost_estimate=pl.CostEstimate(
                flops=flops, bytes_accessed=flops // 64, transcendentals=0
            ),
        )(*inputs)

    def in_vmem(array):
        return pltpu.with_memory_space_constraint(array, pltpu.VMEM)

    def in_hbm(array):
        return pltpu.with_memory_space_constraint(array, pltpu.HBM)

    span, length = span_index[:, None], prefix_len[:, None]
    (carried,) = kernel(
        carry_kernel,
        [span, in_hbm(residual[0]), in_hbm(pending[0])],
        [pltpu.VMEM((tokens, width + HD), bf16)],
        16,
    )
    earlier = to_next_section(carried)
    cache_z = swapped(prefix_cache[0], 2)
    (normed,) = kernel(
        norm_kernel,
        [in_hbm(residual[0]), in_vmem(earlier), in_hbm(norm_gain)],
        [pltpu.HBM((chips, 2 * tokens, width), bf16)],
        16,
    )
    normed, cache_z = after(normed, cache_z)
    gathered = lax.all_to_all(normed, "tp", 0, 0, axis_index_groups=same_core)
    gathered = gathered.reshape(2 * rows, width)

    _, late_earlier = after(normed, earlier)
    (table,) = kernel(
        table_kernel,
        [info, span, late_earlier, cos_tok, sin_tok, cos_span, sin_span],
        [jax.ShapeDtypeStruct((2, 2, rows, HD), f32)],
        16,
        flops=0,
    )
    _, pair_weight, own_w_query, own_w_out, cache_own, cache_z = after(
        normed, jnp.transpose(w_kv[0]), w_query[0], w_out[0], prefix_cache[0], cache_z
    )
    other_pair_weight = swapped(pair_weight, 1)
    other_w_query = swapped(own_w_query, 1)
    caches = [cache_own, cache_z, swapped(cache_own, 1), swapped(cache_z, 1)]
    other_w_out = swapped(own_w_out, 1)

    (pairs,) = kernel(
        pair_kernel,
        [info, gathered, in_hbm(pair_weight), in_hbm(other_pair_weight), table],
        [pltpu.HBM((4, 2, rows, HD), bf16)],
        24,
        2 * 10**9,
    )
    pairs = lax.all_to_all(pairs, "tp", 0, 0, axis_index_groups=same_head)
    anywhere = pl.BlockSpec(memory_space=pl.ANY)
    (queries,) = kernel(
        query_kernel,
        [gathered, in_hbm(own_w_query), in_hbm(other_w_query), table],
        [pltpu.HBM((2, heads * rows, HD), bf16)],
        24,
        4 * rows * heads * HD * width,
        [block(gathered.shape), anywhere, anywhere, block(table.shape)],
        [pltpu.VMEM((2, *own_w_query.shape), bf16), pltpu.SemaphoreType.DMA((heads,))],
    )

    def partial_output(tick):
        pair = block((4, 1, rows, HD), (0, tick, 0, 0))
        far = [in_hbm(array) for array in (queries, *caches, other_w_out)]
        return kernel(
            functools.partial(attend_kernel, tick=tick),
            [info, length, pairs, own_w_out, *far],
            [pltpu.HBM((chips, tokens, width), bf16)],
            24,
            2 * rows * heads * HD * (width + 2 * PREFIX),
            [smem, block(length.shape), pair, block(own_w_out.shape)] + [anywhere] * 6,
            [
                pltpu.VMEM((heads * rows, HD), bf16),
                pltpu.VMEM((4, *cache_own.shape), bf16),
                pltpu.VMEM(own_w_out.shape, bf16),
                pltpu.SemaphoreType.DMA((6,)),
            ],
        )[0]

    def collected(partial):
        partial = lax.all_to_all(partial, "tp", 0, 0, axis_index_groups=same_core)
        return jnp.sum(partial.astype(f32), axis=0).astype(bf16)

    early_output = to_next_section(collected(partial_output(0)))
    output = collected(partial_output(1))
    final_carried = (earlier[:, :width].astype(f32) + early_output.astype(f32)).astype(bf16)
    return (final_carried[None], output[None])


def solution(mesh):
    in_specs = (
        P("segment", "tp", None),
        P("segment", "tp", None),
        P("segment"),
        P("segment"),
        P("segment", None),
        P("segment", None, "tp"),
        P("segment", None, "tp"),
        P("segment", "tp", None),
        P("segment", "tp", None),
    )
    out_specs = (P("segment", "tp", None), P("segment", "tp", None))
    return jax.shard_map(shards, mesh=mesh, in_specs=in_specs, out_specs=out_specs, check_vma=False)
```

```python
import functools

import jax
import jax.numpy as jnp
import numpy as np
from jax import lax
from jax.experimental import pallas as pl
from jax.experimental.pallas import tpu as pltpu
from jax.sharding import PartitionSpec as P

KV_HEADS = 4
HD = 128
SPAN = 128
PREFIX = 1536
SPANS = 64
norm_eps = 1e-05
rope_base = 500000.0
MIB = 1 << 20


contract_last = (((1,), (1,)), ((), ()))


def rope_tables():
    inverse = rope_base ** (-np.arange(0, HD, 2, dtype=np.float64) / HD)
    inverse = np.concatenate([inverse, inverse])
    chips, tokens = SPAN // 16, 8
    place = np.arange(chips)[None, :, None] * 2 + np.arange(2)[:, None, None]
    token = (place * tokens + np.arange(tokens)[None, None, :]).reshape(2, SPAN // 2, 1)
    start = np.arange(SPANS)[:, None] * SPAN
    return [
        np.asarray(f(p * inverse), np.float32) for p in (token, start) for f in (np.cos, np.sin)
    ]


def carry_kernel(span_ref, residual_ref, pending_ref, out_ref):
    tokens, width = residual_ref.shape
    carried = residual_ref[...].astype(jnp.float32) + pending_ref[...].astype(jnp.float32)
    out_ref[:, :width] = carried.astype(jnp.bfloat16)
    index = span_ref[...].astype(jnp.float32).astype(jnp.bfloat16)
    out_ref[:, width:] = jnp.broadcast_to(index, (tokens, out_ref.shape[1] - width))


def normalised(rows_ref, gain_ref):
    rows = rows_ref[:, : gain_ref.shape[1]].astype(jnp.float32)
    mean_square = jnp.mean(rows * rows, axis=-1, keepdims=True)
    return rows * lax.rsqrt(mean_square + norm_eps) * gain_ref[...].astype(jnp.float32)


def norm_kernel(residual_ref, earlier_ref, gain_ref, out_ref):
    ticks = [normalised(ref, gain_ref) for ref in (residual_ref, earlier_ref)]
    normed = jnp.concatenate(ticks, axis=0).astype(jnp.bfloat16)
    for copy in range(out_ref.shape[0]):
        out_ref[copy] = normed


def table_kernel(
    info_ref, span_ref, length_ref, earlier_ref, cos_tok, sin_tok, cos_span, sin_span, out_ref, slots_ref
):
    slots_ref[...] = jnp.broadcast_to(length_ref[...], slots_ref.shape)
    core = info_ref[0]
    late = earlier_ref[:, -HD:].astype(jnp.float32)[:1].astype(jnp.int32)
    spans = lax.broadcasted_iota(jnp.int32, cos_span.shape, 0)
    low = lax.broadcasted_iota(jnp.int32, out_ref.shape[2:], 1) < HD // 2
    cos_b, sin_b = cos_tok[core], sin_tok[core]
    for tick, index in enumerate((span_ref[...], late)):
        cos_a, sin_a = [
            jnp.sum(jnp.where(spans == index, table[...], 0.0), axis=0, keepdims=True)
            for table in (cos_span, sin_span)
        ]
        sine = sin_b * cos_a + cos_b * sin_a
        out_ref[0, tick] = cos_b * cos_a - sin_b * sin_a
        out_ref[1, tick] = jnp.where(low, -sine, sine)


def of_tick(values, tick):
    rows = values.shape[0] // 2
    return values.reshape(rows // 8, 2, 8, HD)[:, tick].reshape(rows, HD)


def rotated(values, table_ref, tick):
    turned = pltpu.roll(values, HD // 2, 1) * table_ref[1, tick]
    return (values * table_ref[0, tick] + turned).astype(jnp.bfloat16)


def query_kernel(rows_ref, own_hbm, other_hbm, table_ref, q_ref, weight_ref, sems):
    sides, steps = sems.shape
    depth = weight_ref.shape[1] // steps
    copies = []
    for side, weight_hbm in enumerate((own_hbm, other_hbm)):
        for step in range(steps):
            part = pl.ds(step * depth, depth)
            copies.append(
                pltpu.make_async_copy(
                    weight_hbm.at[part], weight_ref.at[side, part], sems.at[side, step]
                )
            )
            copies[-1].start()
    rows = rows_ref.shape[0] // 2
    for side in range(sides):
        queries = 0.0
        for step in range(steps):
            part = pl.ds(step * depth, depth)
            copies[side * steps + step].wait()
            queries += jnp.dot(
                rows_ref[:, part], weight_ref[side, part], preferred_element_type=jnp.float32
            )
        heads = queries.shape[1] // HD
        for tick in range(2):
            for head in range(heads):
                values = of_tick(queries[:, head * HD : (head + 1) * HD], tick)
                there = pl.ds((side * heads + head) * rows, rows)
                q_ref[tick, there, :] = rotated(values, table_ref, tick)


def pair_kernel(info_ref, rows_ref, own_ref, other_ref, table_ref, kv_ref):
    core, z_place = info_ref[0], info_ref[1]
    weight = jnp.concatenate([own_ref[...], other_ref[...]], axis=0)
    pairs = lax.dot_general(
        rows_ref[...], weight, contract_last, preferred_element_type=jnp.float32
    )
    pairs = jnp.where(core == 0, pairs, pltpu.roll(pairs, HD // 2, 1))
    for tick in range(2):
        both = of_tick(pairs, tick).astype(jnp.bfloat16)
        keys = rotated(both.astype(jnp.float32), table_ref, tick)
        for copy in range(kv_ref.shape[0]):
            kv_ref[copy, tick] = jnp.where(z_place == 0, keys, both)


def attend_kernel(
    info_ref, slots_ref, kv_ref, wout_own, q_hbm, own, from_z, from_core, from_both, wout_hbm,
    out_hbm, q_ref, cache_ref, wout_other, out_ref, sems, out_sems, *, tick,
):
    copies = [pltpu.make_async_copy(q_hbm.at[tick], q_ref, sems.at[0])]
    for at, cache in enumerate((own, from_z, from_core, from_both)):
        copies.append(pltpu.make_async_copy(cache, cache_ref.at[at], sems.at[1 + at]))
    depth = wout_other.shape[0] // 4
    for at in range(4):
        part = pl.ds(at * depth, depth)
        copies.append(pltpu.make_async_copy(wout_hbm.at[part], wout_other.at[part], sems.at[5 + at]))
    for copy in copies:
        copy.start()
    for copy in copies[:5]:
        copy.wait()
    core, z_place = info_ref[0], info_ref[1]
    chips, tokens, width = out_ref.shape
    rows = chips * tokens
    queries = q_ref[...]

    def token(index, side):
        return ((index % rows // tokens) * 2 + side) * tokens + index % tokens

    row_token = token(lax.broadcasted_iota(jnp.int32, (queries.shape[0], 1), 0), core)
    key = lax.broadcasted_iota(jnp.int32, (1, 2 * rows), 1)
    allowed = [token(key, key // rows) <= row_token]
    keys = [jnp.concatenate([kv_ref[0, 0], kv_ref[1, 0]], axis=0)]
    values = [jnp.concatenate([kv_ref[2, 0], kv_ref[3, 0]], axis=0)]
    block = cache_ref.shape[1]
    slot = lax.broadcasted_iota(jnp.int32, (1, block), 1)
    places = [(z, c) for c in (core, 1 - core) for z in (z_place, 1 - z_place)]
    for at, (z, c) in enumerate(places):
        keys.append(cache_ref[at, :, :HD])
        values.append(cache_ref[at, :, HD:])
        allowed.append((z * 2 + c) * block + slot < slots_ref[:1, :1])

    scores = []
    for key, seen in zip(keys, allowed):
        score = lax.dot_general(queries, key, contract_last, preferred_element_type=jnp.float32)
        scores.append(jnp.where(seen, score * HD ** (-0.5), -jnp.inf))
    peak = functools.reduce(jnp.maximum, [jnp.max(s, axis=-1, keepdims=True) for s in scores])
    total, summed = 0.0, 0.0
    for score, value in zip(scores, values):
        weights = jnp.exp(score - peak)
        total += jnp.sum(weights, axis=-1, keepdims=True)
        summed += jnp.dot(weights.astype(jnp.bfloat16), value, preferred_element_type=jnp.float32)
    result = (summed / total).astype(jnp.bfloat16)
    heads = [result[at : at + rows] for at in range(0, queries.shape[0], rows)]
    half = len(heads) // 2
    sides = [jnp.concatenate(heads[:half], axis=1), jnp.concatenate(heads[half:], axis=1)]
    for copy in copies[5:]:
        copy.wait()
    steps = out_sems.shape[0]
    step = width // steps
    out_copies = []
    for at in range(steps):
        columns = pl.ds(at * step, step)
        part = sum(
            jnp.dot(side, wout_ref[:, columns], preferred_element_type=jnp.float32)
            for side, wout_ref in zip(sides, (wout_own, wout_other))
        )
        out_ref[:, :, columns] = part.reshape(chips, tokens, step).astype(jnp.bfloat16)
        out_copies.append(
            pltpu.make_async_copy(
                out_ref.at[:, :, columns], out_hbm.at[:, :, columns], out_sems.at[at]
            )
        )
        out_copies[at].start()
    for copy in out_copies:
        copy.wait()


def swapped(array, bit):
    return lax.ppermute(array, "tp", [(i, i ^ bit) for i in range(lax.axis_size("tp"))])


def to_next_section(array):
    sections = lax.axis_size("segment")
    return lax.ppermute(array, "segment", [(i, i + 1) for i in range(sections - 1)])


def after(*arrays):
    return lax.optimization_barrier(arrays)


def shards(
    residual, pending, span_index, prefix_len, norm_gain, w_query, w_kv, w_out, prefix_cache
):
    tp_size = lax.axis_size("tp")
    tp_place = lax.axis_index("tp")
    info = jnp.stack([tp_place % 2, tp_place // 2 % 2])
    tokens, width = residual.shape[1:]
    chips = tp_size // 2
    rows = chips * tokens
    local = w_query.shape[2]
    heads = 2 * local // HD
    same_core = [list(range(c, tp_size, 2)) for c in range(2)]
    same_head = [list(range(i, i + 4)) for i in range(0, tp_size, 4)]
    smem = pl.BlockSpec(memory_space=pltpu.SMEM)
    bf16, f32 = jnp.bfloat16, jnp.float32
    cos_tok, sin_tok, cos_span, sin_span = [jnp.asarray(t) for t in rope_tables()]

    def block(shape, place=None):
        place = place or (0,) * len(shape)
        return pl.BlockSpec(shape, lambda step: place)

    def kernel(body, inputs, outs, limit, flops=1 << 20, specs=None, scratch=(), places=None):
        specs = specs or [smem if a.ndim == 1 else block(a.shape) for a in inputs]
        return pl.pallas_call(
            body,
            grid=(1,),
            out_shape=outs,
            in_specs=specs,
            out_specs=places or [block(out.shape) for out in outs],
            scratch_shapes=scratch,
            compiler_params=pltpu.CompilerParams(vmem_limit_bytes=limit * MIB),
            cost_estimate=pl.CostEstimate(
                flops=flops, bytes_accessed=flops // 64, transcendentals=0
            ),
        )(*inputs)

    def in_vmem(array):
        return pltpu.with_memory_space_constraint(array, pltpu.VMEM)

    def in_hbm(array):
        return pltpu.with_memory_space_constraint(array, pltpu.HBM)

    span, length = span_index[:, None], prefix_len[:, None]
    (carried,) = kernel(
        carry_kernel,
        [span, in_hbm(residual[0]), in_hbm(pending[0])],
        [pltpu.VMEM((tokens, width + HD), bf16)],
        16,
    )
    earlier = to_next_section(carried)
    cache_z = swapped(prefix_cache[0], 2)
    (normed,) = kernel(
        norm_kernel,
        [in_hbm(residual[0]), in_vmem(earlier), in_hbm(norm_gain)],
        [pltpu.HBM((chips, 2 * tokens, width), bf16)],
        16,
        10 * 10**9,
    )
    normed, cache_z = after(normed, cache_z)
    gathered = lax.all_to_all(normed, "tp", 0, 0, axis_index_groups=same_core)
    gathered = gathered.reshape(2 * rows, width)

    _, late_earlier = after(normed, earlier)
    table, slots = kernel(
        table_kernel,
        [info, span, length, late_earlier]
        + [in_hbm(constant) for constant in (cos_tok, sin_tok, cos_span, sin_span)],
        [jax.ShapeDtypeStruct((2, 2, rows, HD), f32), jax.ShapeDtypeStruct((8, HD), jnp.int32)],
        16,
        flops=0,
    )
    _, pair_weight, own_w_query, own_w_out, cache_own, cache_z = after(
        normed, jnp.transpose(w_kv[0]), w_query[0], w_out[0], prefix_cache[0], cache_z
    )
    other_pair_weight = swapped(pair_weight, 1)
    other_w_query = swapped(own_w_query, 1)
    caches = [cache_own, cache_z, swapped(cache_own, 1), swapped(cache_z, 1)]
    other_w_out = swapped(own_w_out, 1)

    (pairs,) = kernel(
        pair_kernel,
        [info, gathered, in_hbm(pair_weight), in_hbm(other_pair_weight), table],
        [pltpu.HBM((4, 2, rows, HD), bf16)],
        24,
        2 * 10**9,
    )
    pairs = lax.all_to_all(pairs, "tp", 0, 0, axis_index_groups=same_head)
    anywhere = pl.BlockSpec(memory_space=pl.ANY)
    (queries,) = kernel(
        query_kernel,
        [gathered, in_hbm(own_w_query), in_hbm(other_w_query), table],
        [pltpu.HBM((2, heads * rows, HD), bf16)],
        24,
        4 * rows * heads * HD * width,
        [block(gathered.shape), anywhere, anywhere, block(table.shape)],
        [pltpu.VMEM((2, *own_w_query.shape), bf16), pltpu.SemaphoreType.DMA((2, 4))],
    )

    def partial_output(tick):
        pair = block((4, 1, rows, HD), (0, tick, 0, 0))
        far = [in_hbm(array) for array in (queries, *caches, other_w_out)]
        return kernel(
            functools.partial(attend_kernel, tick=tick),
            [info, slots, pairs, own_w_out, *far],
            [pltpu.HBM((chips, tokens, width), bf16)],
            24,
            2 * rows * heads * HD * (width + 2 * PREFIX),
            [smem, block(slots.shape), pair, block(own_w_out.shape)] + [anywhere] * 6,
            [
                pltpu.VMEM((heads * rows, HD), bf16),
                pltpu.VMEM((4, *cache_own.shape), bf16),
                pltpu.VMEM(own_w_out.shape, bf16),
                pltpu.VMEM((chips, tokens, width), bf16),
                pltpu.SemaphoreType.DMA((9,)),
                pltpu.SemaphoreType.DMA((4,)),
            ],
            [anywhere],
        )[0]

    def collected(partial):
        partial = lax.all_to_all(partial, "tp", 0, 0, axis_index_groups=same_core)
        return jnp.sum(partial.astype(f32), axis=0).astype(bf16)

    early_output = to_next_section(collected(partial_output(0)))
    output = collected(partial_output(1))
    final_carried = (earlier[:, :width].astype(f32) + early_output.astype(f32)).astype(bf16)
    return (final_carried[None], output[None])


def solution(mesh):
    in_specs = (
        P("segment", "tp", None),
        P("segment", "tp", None),
        P("segment"),
        P("segment"),
        P("segment", None),
        P("segment", None, "tp"),
        P("segment", None, "tp"),
        P("segment", "tp", None),
        P("segment", "tp", None),
    )
    out_specs = (P("segment", "tp", None), P("segment", "tp", None))
    return jax.shard_map(shards, mesh=mesh, in_specs=in_specs, out_specs=out_specs, check_vma=False)
```

```python
import functools

import jax
import jax.numpy as jnp
import numpy as np
from jax import lax
from jax.experimental import pallas as pl
from jax.experimental.pallas import tpu as pltpu
from jax.sharding import PartitionSpec as P

KV_HEADS = 4
HD = 128
SPAN = 128
PREFIX = 1536
SPANS = 64
norm_eps = 1e-05
rope_base = 500000.0
MIB = 1 << 20


contract_last = (((1,), (1,)), ((), ()))


def rope_tables():
    inverse = rope_base ** (-np.arange(0, HD, 2, dtype=np.float64) / HD)
    inverse = np.concatenate([inverse, inverse])
    chips, tokens = SPAN // 16, 8
    place = np.arange(chips)[None, :, None] * 2 + np.arange(2)[:, None, None]
    token = (place * tokens + np.arange(tokens)[None, None, :]).reshape(2, SPAN // 2, 1)
    start = np.arange(SPANS)[:, None] * SPAN
    return [
        np.asarray(f(p * inverse), np.float32) for p in (token, start) for f in (np.cos, np.sin)
    ]


def carry_kernel(span_ref, residual_ref, pending_ref, out_ref):
    tokens, width = residual_ref.shape
    carried = residual_ref[...].astype(jnp.float32) + pending_ref[...].astype(jnp.float32)
    out_ref[:, :width] = carried.astype(jnp.bfloat16)
    index = span_ref[...].astype(jnp.float32).astype(jnp.bfloat16)
    out_ref[:, width:] = jnp.broadcast_to(index, (tokens, out_ref.shape[1] - width))


def normalised(rows, gain):
    mean_square = jnp.mean(rows * rows, axis=-1, keepdims=True)
    return rows * lax.rsqrt(mean_square + norm_eps) * gain


def early_norm_kernel(residual_ref, gain_ref, out_ref, wide_gain_ref):
    gain = gain_ref[...].astype(jnp.float32)
    wide_gain_ref[...] = gain
    out_ref[...] = normalised(residual_ref[...].astype(jnp.float32), gain)


def norm_kernel(early_ref, earlier_ref, gain_ref, out_ref):
    rows = earlier_ref[:, : gain_ref.shape[1]].astype(jnp.float32)
    ticks = [early_ref[...], normalised(rows, gain_ref[...])]
    normed = jnp.concatenate(ticks, axis=0).astype(jnp.bfloat16)
    for copy in range(out_ref.shape[0]):
        out_ref[copy] = normed


def table_kernel(
    info_ref, span_ref, length_ref, earlier_ref, cos_tok, sin_tok, cos_span, sin_span, out_ref, slots_ref
):
    slots_ref[...] = jnp.broadcast_to(length_ref[...], slots_ref.shape)
    core = info_ref[0]
    late = earlier_ref[:, -HD:].astype(jnp.float32)[:1].astype(jnp.int32)
    spans = lax.broadcasted_iota(jnp.int32, cos_span.shape, 0)
    low = lax.broadcasted_iota(jnp.int32, out_ref.shape[2:], 1) < HD // 2
    cos_b, sin_b = cos_tok[core], sin_tok[core]
    for tick, index in enumerate((span_ref[...], late)):
        cos_a, sin_a = [
            jnp.sum(jnp.where(spans == index, table[...], 0.0), axis=0, keepdims=True)
            for table in (cos_span, sin_span)
        ]
        sine = sin_b * cos_a + cos_b * sin_a
        out_ref[0, tick] = cos_b * cos_a - sin_b * sin_a
        out_ref[1, tick] = jnp.where(low, -sine, sine)


def of_tick(values, tick):
    rows = values.shape[0] // 2
    return values.reshape(rows // 8, 2, 8, HD)[:, tick].reshape(rows, HD)


def rotated(values, table_ref, tick):
    turned = pltpu.roll(values, HD // 2, 1) * table_ref[1, tick]
    return (values * table_ref[0, tick] + turned).astype(jnp.bfloat16)


def query_kernel(rows_ref, own_hbm, other_hbm, table_ref, q_ref, weight_ref, sems):
    sides, steps = sems.shape
    depth = weight_ref.shape[1] // steps
    copies = []
    for side, weight_hbm in enumerate((own_hbm, other_hbm)):
        for step in range(steps):
            part = pl.ds(step * depth, depth)
            copies.append(
                pltpu.make_async_copy(
                    weight_hbm.at[part], weight_ref.at[side, part], sems.at[side, step]
                )
            )
            copies[-1].start()
    rows = rows_ref.shape[0] // 2
    for side in range(sides):
        queries = 0.0
        for step in range(steps):
            part = pl.ds(step * depth, depth)
            copies[side * steps + step].wait()
            queries += jnp.dot(
                rows_ref[:, part], weight_ref[side, part], preferred_element_type=jnp.float32
            )
        heads = queries.shape[1] // HD
        for tick in range(2):
            for head in range(heads):
                values = of_tick(queries[:, head * HD : (head + 1) * HD], tick)
                there = pl.ds((side * heads + head) * rows, rows)
                q_ref[tick, there, :] = rotated(values, table_ref, tick)


def pair_kernel(info_ref, rows_ref, own_ref, other_ref, table_ref, kv_ref):
    core, z_place = info_ref[0], info_ref[1]
    weight = jnp.concatenate([own_ref[...], other_ref[...]], axis=0)
    pairs = lax.dot_general(
        rows_ref[...], weight, contract_last, preferred_element_type=jnp.float32
    )
    pairs = jnp.where(core == 0, pairs, pltpu.roll(pairs, HD // 2, 1))
    for tick in range(2):
        both = of_tick(pairs, tick).astype(jnp.bfloat16)
        keys = rotated(both.astype(jnp.float32), table_ref, tick)
        for copy in range(kv_ref.shape[0]):
            kv_ref[copy, tick] = jnp.where(z_place == 0, keys, both)


def attend_kernel(
    info_ref, slots_ref, kv_ref, wout_own, q_hbm, own, from_z, from_core, from_both, wout_hbm,
    out_hbm, q_ref, cache_ref, wout_other, out_ref, sems, out_sems, *, tick,
):
    copies = [pltpu.make_async_copy(q_hbm.at[tick], q_ref, sems.at[0])]
    for at, cache in enumerate((own, from_z, from_core, from_both)):
        copies.append(pltpu.make_async_copy(cache, cache_ref.at[at], sems.at[1 + at]))
    depth = wout_other.shape[0] // 4
    for at in range(4):
        part = pl.ds(at * depth, depth)
        copies.append(pltpu.make_async_copy(wout_hbm.at[part], wout_other.at[part], sems.at[5 + at]))
    for copy in copies:
        copy.start()
    for copy in copies[:5]:
        copy.wait()
    core, z_place = info_ref[0], info_ref[1]
    chips, tokens, width = out_ref.shape
    rows = chips * tokens
    queries = q_ref[...]

    def token(index, side):
        return ((index % rows // tokens) * 2 + side) * tokens + index % tokens

    row_token = token(lax.broadcasted_iota(jnp.int32, (queries.shape[0], 1), 0), core)
    key = lax.broadcasted_iota(jnp.int32, (1, 2 * rows), 1)
    allowed = [token(key, key // rows) <= row_token]
    keys = [jnp.concatenate([kv_ref[0, 0], kv_ref[1, 0]], axis=0)]
    values = [jnp.concatenate([kv_ref[2, 0], kv_ref[3, 0]], axis=0)]
    block = cache_ref.shape[1]
    slot = lax.broadcasted_iota(jnp.int32, (1, block), 1)
    places = [(z, c) for c in (core, 1 - core) for z in (z_place, 1 - z_place)]
    for at, (z, c) in enumerate(places):
        keys.append(cache_ref[at, :, :HD])
        values.append(cache_ref[at, :, HD:])
        allowed.append((z * 2 + c) * block + slot < slots_ref[:1, :1])

    scores = []
    for key, seen in zip(keys, allowed):
        score = lax.dot_general(queries, key, contract_last, preferred_element_type=jnp.float32)
        scores.append(jnp.where(seen, score * HD ** (-0.5), -jnp.inf))
    peak = functools.reduce(jnp.maximum, [jnp.max(s, axis=-1, keepdims=True) for s in scores])
    total, summed = 0.0, 0.0
    for score, value in zip(scores, values):
        weights = jnp.exp(score - peak)
        total += jnp.sum(weights, axis=-1, keepdims=True)
        summed += jnp.dot(weights.astype(jnp.bfloat16), value, preferred_element_type=jnp.float32)
    result = (summed / total).astype(jnp.bfloat16)
    heads = [result[at : at + rows] for at in range(0, queries.shape[0], rows)]
    half = len(heads) // 2
    sides = [jnp.concatenate(heads[:half], axis=1), jnp.concatenate(heads[half:], axis=1)]
    for copy in copies[5:]:
        copy.wait()
    steps = out_sems.shape[0]
    step = width // steps
    out_copies = []
    for at in range(steps):
        columns = pl.ds(at * step, step)
        part = sum(
            jnp.dot(side, wout_ref[:, columns], preferred_element_type=jnp.float32)
            for side, wout_ref in zip(sides, (wout_own, wout_other))
        )
        out_ref[:, :, columns] = part.reshape(chips, tokens, step).astype(jnp.bfloat16)
        out_copies.append(
            pltpu.make_async_copy(
                out_ref.at[:, :, columns], out_hbm.at[:, :, columns], out_sems.at[at]
            )
        )
        out_copies[at].start()
    for copy in out_copies:
        copy.wait()


def swapped(array, bit):
    return lax.ppermute(array, "tp", [(i, i ^ bit) for i in range(lax.axis_size("tp"))])


def to_next_section(array):
    sections = lax.axis_size("segment")
    return lax.ppermute(array, "segment", [(i, i + 1) for i in range(sections - 1)])


def after(*arrays):
    return lax.optimization_barrier(arrays)


def shards(
    residual, pending, span_index, prefix_len, norm_gain, w_query, w_kv, w_out, prefix_cache
):
    tp_size = lax.axis_size("tp")
    tp_place = lax.axis_index("tp")
    info = jnp.stack([tp_place % 2, tp_place // 2 % 2])
    tokens, width = residual.shape[1:]
    chips = tp_size // 2
    rows = chips * tokens
    local = w_query.shape[2]
    heads = 2 * local // HD
    same_core = [list(range(c, tp_size, 2)) for c in range(2)]
    same_head = [list(range(i, i + 4)) for i in range(0, tp_size, 4)]
    smem = pl.BlockSpec(memory_space=pltpu.SMEM)
    bf16, f32 = jnp.bfloat16, jnp.float32
    cos_tok, sin_tok, cos_span, sin_span = [jnp.asarray(t) for t in rope_tables()]

    def block(shape, place=None):
        place = place or (0,) * len(shape)
        return pl.BlockSpec(shape, lambda step: place)

    def kernel(body, inputs, outs, limit, flops=1 << 20, specs=None, scratch=(), places=None):
        specs = specs or [smem if a.ndim == 1 else block(a.shape) for a in inputs]
        return pl.pallas_call(
            body,
            grid=(1,),
            out_shape=outs,
            in_specs=specs,
            out_specs=places or [block(out.shape) for out in outs],
            scratch_shapes=scratch,
            compiler_params=pltpu.CompilerParams(vmem_limit_bytes=limit * MIB),
            cost_estimate=pl.CostEstimate(
                flops=flops, bytes_accessed=flops // 64, transcendentals=0
            ),
        )(*inputs)

    def in_vmem(array):
        return pltpu.with_memory_space_constraint(array, pltpu.VMEM)

    def in_hbm(array):
        return pltpu.with_memory_space_constraint(array, pltpu.HBM)

    span, length = span_index[:, None], prefix_len[:, None]
    (carried,) = kernel(
        carry_kernel,
        [span, in_hbm(residual[0]), in_hbm(pending[0])],
        [pltpu.VMEM((tokens, width + HD), bf16)],
        16,
    )
    earlier = to_next_section(carried)
    cache_z = swapped(prefix_cache[0], 2)
    early_normed, wide_gain = kernel(
        early_norm_kernel,
        [in_hbm(residual[0]), in_hbm(norm_gain)],
        [pltpu.VMEM((tokens, width), f32), pltpu.VMEM((1, width), f32)],
        16,
    )
    (normed,) = kernel(
        norm_kernel,
        [in_vmem(early_normed), in_vmem(earlier), in_vmem(wide_gain)],
        [pltpu.HBM((chips, 2 * tokens, width), bf16)],
        16,
        10 * 10**9,
    )
    normed, cache_z = after(normed, cache_z)
    gathered = lax.all_to_all(normed, "tp", 0, 0, axis_index_groups=same_core)
    gathered = gathered.reshape(2 * rows, width)

    _, late_earlier = after(normed, earlier)
    table, slots = kernel(
        table_kernel,
        [info, span, length, late_earlier]
        + [in_hbm(constant) for constant in (cos_tok, sin_tok, cos_span, sin_span)],
        [jax.ShapeDtypeStruct((2, 2, rows, HD), f32), jax.ShapeDtypeStruct((8, HD), jnp.int32)],
        16,
        flops=0,
    )
    _, pair_weight, own_w_query, own_w_out, cache_own, cache_z = after(
        normed, jnp.transpose(w_kv[0]), w_query[0], w_out[0], prefix_cache[0], cache_z
    )
    other_pair_weight = swapped(pair_weight, 1)
    other_w_query = swapped(own_w_query, 1)
    caches = [cache_own, cache_z, swapped(cache_own, 1), swapped(cache_z, 1)]
    other_w_out = swapped(own_w_out, 1)

    (pairs,) = kernel(
        pair_kernel,
        [info, gathered, in_hbm(pair_weight), in_hbm(other_pair_weight), table],
        [pltpu.HBM((4, 2, rows, HD), bf16)],
        24,
        2 * 10**9,
    )
    pairs = lax.all_to_all(pairs, "tp", 0, 0, axis_index_groups=same_head)
    anywhere = pl.BlockSpec(memory_space=pl.ANY)
    (queries,) = kernel(
        query_kernel,
        [gathered, in_hbm(own_w_query), in_hbm(other_w_query), table],
        [pltpu.HBM((2, heads * rows, HD), bf16)],
        24,
        4 * rows * heads * HD * width,
        [block(gathered.shape), anywhere, anywhere, block(table.shape)],
        [pltpu.VMEM((2, *own_w_query.shape), bf16), pltpu.SemaphoreType.DMA((2, 4))],
    )

    def partial_output(tick):
        pair = block((4, 1, rows, HD), (0, tick, 0, 0))
        far = [in_hbm(array) for array in (queries, *caches, other_w_out)]
        return kernel(
            functools.partial(attend_kernel, tick=tick),
            [info, slots, pairs, own_w_out, *far],
            [pltpu.HBM((chips, tokens, width), bf16)],
            24,
            2 * rows * heads * HD * (width + 2 * PREFIX),
            [smem, block(slots.shape), pair, block(own_w_out.shape)] + [anywhere] * 6,
            [
                pltpu.VMEM((heads * rows, HD), bf16),
                pltpu.VMEM((4, *cache_own.shape), bf16),
                pltpu.VMEM(own_w_out.shape, bf16),
                pltpu.VMEM((chips, tokens, width), bf16),
                pltpu.SemaphoreType.DMA((9,)),
                pltpu.SemaphoreType.DMA((4,)),
            ],
            [anywhere],
        )[0]

    def collected(partial):
        partial = lax.all_to_all(partial, "tp", 0, 0, axis_index_groups=same_core)
        return jnp.sum(partial.astype(f32), axis=0).astype(bf16)

    early_output = to_next_section(collected(partial_output(0)))
    output = collected(partial_output(1))
    final_carried = (earlier[:, :width].astype(f32) + early_output.astype(f32)).astype(bf16)
    return (final_carried[None], output[None])


def solution(mesh):
    in_specs = (
        P("segment", "tp", None),
        P("segment", "tp", None),
        P("segment"),
        P("segment"),
        P("segment", None),
        P("segment", None, "tp"),
        P("segment", None, "tp"),
        P("segment", "tp", None),
        P("segment", "tp", None),
    )
    out_specs = (P("segment", "tp", None), P("segment", "tp", None))
    return jax.shard_map(shards, mesh=mesh, in_specs=in_specs, out_specs=out_specs, check_vma=False)
```
